256 devices in a mesh: expert: 64 (over x, z, core), etp: 4 (over y).
Axes of the slice: x: 4, y: 4, z: 8, core: 2. Of those that a mesh axis runs over, the one named last changes fastest.
Arguments:
- tokens: bfloat16 [2048, 7168], P('expert'), may hold values from -6 to 6
- out_grad: bfloat16 [2048, 7168], P('expert'), may hold values from -1.5 to 1.5
- routes: int32 [2048, 8], P('expert'), may hold values from 0 to 63, all different within a row; in each aligned block of 32 rows (0 to 31, 32 to 63, ...) at most 5 rows name the same one
- gates: bfloat16 [2048, 8], P('expert'), may hold values from 0.099609375 to 1
- w_gate: bfloat16 [64, 7168, 1024], P('expert', None, 'etp'), may hold values from -0.0625 to 0.0625
- w_up: bfloat16 [64, 7168, 1024], P('expert', None, 'etp'), may hold values from -0.0625 to 0.0625
- w_down: bfloat16 [64, 1024, 7168], P('expert', 'etp'), may hold values from -0.1875 to 0.1875
Outputs:
- input_grad: bfloat16 [2048, 7168], P('expert', 'etp')
- gate_grad: bfloat16 [2048, 8], P('expert')
The draws below stay inside these ranges and needn't reach their ends.
Inputs may be any that keep to these rules, and one draw needn't show every extreme that they name: `routes`: each token's 8 experts differ; the rows of one index of expert choose any one expert at most 5 times, a bound that some block reaches.
All inputs are finite; a program needn't handle non-finite values.
Results may differ from the reference program's by a relative error of at most 0.0058.
Values may be sent and summed in bfloat16 or wider, within the bound.
No kernel may reach another device: no remote copies, remote signals or barrier semaphores. Data moves between devices by JAX's collectives and lax.ppermute only.
A program may use at most 128 MiB of HBM per device.

```python
import math
import jax
import jax.numpy as jnp
import numpy as np
from jax import lax

D = 7168
FF = 1024
TOP = 8
TOK_DEV = 32
EXPERTS = 64
TOKENS = 2048
CAP = 5
N_EXPERT = 64


def steps_of(own_key, dims, split, least, top_value):
    gain, own = 1.0, jax.random.fold_in(own_key, 6)
    for dim, blocks in split:
        heights = jnp.exp(jax.random.uniform(jax.random.fold_in(own, dim), (blocks,), jnp.float32, least / len(split), top_value / len(split)))
        gain = gain * jnp.repeat(heights, dims[dim] // blocks).reshape([-1 if axis == dim else 1 for axis in range(len(dims))])
    return gain


def assign_block(own_key, own, number, rows, amount, top, reach, lean):
    order = jax.random.permutation(own_key, amount)
    heavy_load, ordinary = load_shares(amount, rows * top, reach, lean, True), load_shares(amount, rows * top, reach, lean, False)
    places = jnp.arange(amount)

    def named(tallies, offset_by):
        used = int((tallies > 0).sum())
        fixed = max(1, used // 4)
        passed = fixed + (places - fixed + offset_by * (used - fixed)) % max(1, amount - fixed)
        return jnp.zeros((amount,), jnp.int32).at[order[jnp.where(places < fixed, places, passed)]].set(jnp.asarray(tallies, jnp.int32))

    tallies = jnp.where(number % 4 == 0, named(heavy_load, number // 4), named(ordinary, number - number // 4 - 1))
    mixed = jax.random.permutation(jax.random.fold_in(own, 3), amount)
    donor, sink = mixed[0:amount // 2 * 2:2], mixed[1:amount // 2 * 2:2]
    margin = jnp.minimum(tallies[donor] - 1, reach - tallies[sink]) // 2
    margin = jnp.where((donor == order[0]) | (sink == order[0]) | (tallies[sink] == 0), 0, jnp.maximum(margin, 0))
    passed = jax.random.randint(jax.random.fold_in(own, 4), (amount // 2,), 0, 1 << 20) % (margin + 1)
    tallies = tallies.at[donor].add(-passed).at[sink].add(passed)
    items = jnp.searchsorted(jnp.cumsum(tallies), jnp.arange(rows * top), side="right").astype(jnp.int32)
    grid = items.reshape(top, rows).T
    grid = grid[jax.random.permutation(jax.random.fold_in(own, 1), rows)]
    offset_by = jax.random.randint(jax.random.fold_in(own, 2), (rows, 1), 0, top)
    return jnp.take_along_axis(grid, (jnp.arange(top)[None, :] + offset_by) % top, axis=1)


def load_shares(count, total, reach, skew, full):
    weights = [(1 << 20) // math.isqrt(standing ** skew) + 1 for standing in range(1, count + 1)]
    largest = reach if full else min(reach, max(-(-total // count), total * weights[0] // sum(weights)))
    least = 1 if total - largest >= count - 1 else 0
    counts, rest = [largest] + [least] * (count - 1), total - largest - least * (count - 1)
    while rest > 0:
        free = [i for i in range(1, count) if counts[i] < largest] or [i for i in range(1, count) if counts[i] < reach]
        mass, left = sum([weights[i] for i in free]), rest
        for i in free:
            more = min(reach - counts[i], max(1, left * weights[i] // mass), rest)
            counts[i] = counts[i] + more
            rest = rest - more
    return np.array(counts)


def centred(key, shape, width, bound, pieces=(), kind=jnp.bfloat16):
    result = jax.random.normal(key, shape, jnp.float32) * width
    if len(pieces) > 0:
        result = steps_of(key, shape, pieces, -0.22, 0.18) * result
    return jnp.clip(result, min=-bound, max=bound).astype(kind)


def setup_inputs(seed: int = 0) -> dict:
    keys = jax.random.split(jax.random.key(seed), 8)
    tokens = centred(keys[0], (TOKENS, D), 1.0, 6.0, ((0, 64),))
    out_grad = centred(keys[1], (TOKENS, D), 0.25, 1.5, ((0, 64),))
    routes_keys = jax.random.split(jax.random.fold_in(keys[2], 1), TOKENS // TOK_DEV)
    routes_turns = jax.random.permutation(jax.random.fold_in(keys[2], 3), TOKENS // TOK_DEV)
    routes = jax.vmap(lambda own, number: assign_block(jax.random.fold_in(keys[2], 2), own, number, TOK_DEV, EXPERTS, TOP, CAP, 2))(routes_keys, routes_turns).reshape((TOKENS, TOP))
    gates = jnp.clip(jnp.exp(math.log(1.0) - 2.306499 * jax.random.uniform(keys[3], (TOKENS, TOP), jnp.float32) ** steps_of(keys[3], (TOKENS, TOP), ((0, 64),), -0.2, 0.2)), 0.099609375, 1.0).astype(jnp.bfloat16)
    w_gate = centred(keys[4], (EXPERTS, D, FF), D ** -0.5, 0.0625, ((0, 64), (2, 4)))
    w_up = centred(keys[5], (EXPERTS, D, FF), D ** -0.5, 0.0625, ((0, 64), (2, 4)))
    w_down = centred(keys[6], (EXPERTS, FF, D), FF ** -0.5, 0.1875, ((0, 64), (1, 4)))
    return dict(tokens=tokens, out_grad=out_grad, routes=routes, gates=gates, w_gate=w_gate, w_up=w_up, w_down=w_down)


def slot_backward(inputs, grads, gate_vals, wgate, wup, wdown):
    pre_gate = jnp.dot(inputs, wgate, preferred_element_type=jnp.float32)
    pre_up = jnp.dot(inputs, wup, preferred_element_type=jnp.float32)
    sigma = jax.nn.sigmoid(pre_gate)
    silu_val = pre_gate * sigma
    act = (silu_val * pre_up).astype(jnp.bfloat16)
    expert_out = jnp.dot(act, wdown, preferred_element_type=jnp.float32)
    gate_part = jnp.sum(grads.astype(jnp.float32) * expert_out, axis=1)
    grad_act = jnp.dot(grads, wdown.T, preferred_element_type=jnp.float32)
    grad_act = grad_act * gate_vals.astype(jnp.float32)[:, None]
    grad_gate = (grad_act * pre_up * sigma * (1.0 + pre_gate * (1.0 - sigma))).astype(jnp.bfloat16)
    grad_up = (grad_act * silu_val).astype(jnp.bfloat16)
    input_part = jnp.dot(grad_gate, wgate.T, preferred_element_type=jnp.float32)
    input_part = input_part + jnp.dot(grad_up, wup.T, preferred_element_type=jnp.float32)
    return input_part, gate_part


def reference(tokens, out_grad, routes, gates, w_gate, w_up, w_down):
    flat = routes.reshape(-1).astype(jnp.int32)
    gate_flat = gates.reshape(-1)
    most = N_EXPERT * CAP

    def visit(carry, index):
        total, gate_total = carry
        chosen = flat == index
        slots = jnp.nonzero(chosen, size=most, fill_value=0)[0].astype(jnp.int32)
        count = jnp.sum(chosen.astype(jnp.int32))
        valid = jnp.arange(most, dtype=jnp.int32) < count
        rows_of = (slots // TOP).astype(jnp.int32)
        inputs = jnp.where(valid[:, None], tokens[rows_of], jnp.zeros((), jnp.bfloat16))
        grads = jnp.where(valid[:, None], out_grad[rows_of], jnp.zeros((), jnp.bfloat16))
        gate_vals = jnp.where(valid, gate_flat[slots], jnp.zeros((), jnp.bfloat16))
        input_part, gate_part = slot_backward(inputs, grads, gate_vals, w_gate[index], w_up[index], w_down[index])
        input_round = lax.optimization_barrier(input_part.astype(jnp.bfloat16)).astype(jnp.float32)
        gate_round = lax.optimization_barrier(gate_part.astype(jnp.bfloat16)).astype(jnp.float32)
        total = total.at[rows_of].add(jnp.where(valid[:, None], input_round, jnp.zeros((), jnp.float32)))
        gate_total = gate_total.at[slots].add(jnp.where(valid, gate_round, jnp.zeros((), jnp.float32)))
        return (total, gate_total), None

    start = (jnp.zeros((TOKENS, D), jnp.float32), jnp.zeros((TOKENS * TOP,), jnp.float32))
    (total, gate_total), unused = lax.scan(visit, start, jnp.arange(EXPERTS, dtype=jnp.int32))
    return total.astype(jnp.bfloat16), gate_total.reshape(TOKENS, TOP).astype(jnp.bfloat16)
```

```python
import jax
import jax.numpy as jnp
from jax import lax
from jax.sharding import PartitionSpec as P

BF = jnp.bfloat16
F32 = jnp.float32
NX, NZ, NC, NY = 4, 8, 2, 4
CAP = 5
SHIFTS = ((0, 0), (0, 1), (1, 0), (-1, 0), (1, 1), (-1, 1), (2, 0), (2, 1))
ZS = (0, 1, -1, 2, -2, 3, -3, 4)


def move(value, dx=0, dz=0, dc=0):
    if dx % NX == 0 and dz % NZ == 0 and dc % NC == 0:
        return value
    pairs = []
    for x in range(NX):
        for z in range(NZ):
            for c in range(NC):
                to = (((x + dx) % NX) * NZ + (z + dz) % NZ) * NC + (c + dc) % NC
                pairs.append(((x * NZ + z) * NC + c, to))
    return lax.ppermute(value, "expert", pairs)


def move_y(value, dy):
    return lax.ppermute(value, "etp", [(y, (y + dy) % NY) for y in range(NY)])


def gather_z(value):
    blocks = {0: value}
    up = down = value
    for step in range(1, 5):
        up = move(up, dz=1)
        blocks[step] = up
        if step < 4:
            down = move(down, dz=-1)
            blocks[-step] = down
    return jnp.concatenate([blocks[d] for d in ZS], axis=0)


def dot(a, b):
    return jnp.dot(a, b, preferred_element_type=F32)


def dot_t(a, b):
    return lax.dot_general(a, b, (((1,), (1,)), ((), ())), preferred_element_type=F32)


def on_device(tokens, out_grad, routes, gates, w_gate, w_up, w_down):
    rows, width = tokens.shape
    half, quarter, eighth = width // 2, width // 4, width // 8
    me = lax.axis_index("expert")
    y = lax.axis_index("etp")
    x, z, core = me // (NZ * NC), (me // NC) % NZ, me % NC
    side = y % 2
    wgate, wup, wdown = w_gate[0], w_up[0], w_down[0]

    meta = jnp.concatenate([routes.astype(BF), gates, jnp.zeros((rows, 112), BF)], axis=1)
    tok_half = lax.dynamic_slice(tokens, (0, side * half), (rows, half))
    grad_half = lax.dynamic_slice(out_grad, (0, side * half), (rows, half))
    tok_z = gather_z(jnp.concatenate([tok_half, meta], axis=1))
    grad_z = gather_z(grad_half)

    route_z = tok_z[:, half : half + 8].astype(F32)
    ids = jnp.stack(
        [((x + dx) % NX) * (NZ * NC) + z * NC + (core + dc) % NC for dx, dc in SHIFTS]
    ).astype(F32)
    hit = route_z[:, None, :] == ids[None, :, None]
    chosen = jnp.any(hit, axis=2).astype(F32)
    count = NZ * rows
    spot = jnp.arange(count, dtype=jnp.int32)
    before = ((spot[:, None] // rows == spot[None, :] // rows) & (spot[:, None] > spot[None, :])).astype(BF)
    position = dot(before, chosen.astype(BF))
    place = jnp.where(chosen > 0, position, -1.0).T
    slot = jnp.arange(NZ * CAP, dtype=jnp.int32)
    wanted = jnp.where(
        slot[:, None] // CAP == spot[None, :] // rows, (slot[:, None] % CAP).astype(F32), -2.0
    )
    picked = place[:, None, :] == wanted[None, :, :]
    picker = picked.astype(BF).reshape(8 * NZ * CAP, count)

    def send_x(value):
        block = NZ * CAP
        out = []
        for i, (dx, dc) in enumerate(SHIFTS):
            out.append(move(value[i * block : (i + 1) * block], dx=dx, dc=dc))
        return jnp.concatenate(out, axis=0)

    def back_x(value):
        block = NZ * CAP
        out = []
        for i, (dx, dc) in enumerate(SHIFTS):
            out.append(move(value[i * block : (i + 1) * block], dx=-dx, dc=-dc))
        return jnp.concatenate(out, axis=0)

    tok_x = send_x(dot(picker, tok_z).astype(BF))
    grad_x = send_x(dot(picker, grad_z).astype(BF))
    tok_own, meta_x = tok_x[:, :half], tok_x[:, half : half + 16].astype(F32)
    gate_vals = jnp.sum(
        jnp.where(meta_x[:, :8] == me.astype(F32), meta_x[:, 8:], 0.0), axis=1, keepdims=True
    )

    tok_low, tok_high = move_y(tok_own[:, :quarter], 1), move_y(tok_own[:, quarter:], -1)
    grad_low, grad_high = move_y(grad_x[:, :quarter], 1), move_y(grad_x[:, quarter:], -1)
    own_at, low_at = side * half, (1 - side) * half
    high_at = low_at + quarter

    def by_rows(weight):
        total = dot(tok_own, lax.dynamic_slice_in_dim(weight, own_at, half, 0))
        total += dot(tok_low, lax.dynamic_slice_in_dim(weight, low_at, quarter, 0))
        return total + dot(tok_high, lax.dynamic_slice_in_dim(weight, high_at, quarter, 0))

    pre_gate = by_rows(wgate)
    pre_up = by_rows(wup)
    sigma = jax.nn.sigmoid(pre_gate)
    silu_val = pre_gate * sigma
    act = (silu_val * pre_up).astype(BF)
    raw = dot_t(grad_x, lax.dynamic_slice_in_dim(wdown, own_at, half, 1))
    raw += dot_t(grad_low, lax.dynamic_slice_in_dim(wdown, low_at, quarter, 1))
    raw += dot_t(grad_high, lax.dynamic_slice_in_dim(wdown, high_at, quarter, 1))
    gate_sum = jnp.sum(act.astype(F32) * raw, axis=1, keepdims=True)
    gate_sum = gate_sum + lax.ppermute(gate_sum, "etp", [(0, 1), (1, 0), (2, 3), (3, 2)])
    gate_sum = gate_sum + lax.ppermute(gate_sum, "etp", [(0, 2), (1, 3), (2, 0), (3, 1)])
    slot_gate = gate_sum.astype(BF)
    grad_act = raw * gate_vals
    grad_gate = (grad_act * pre_up * sigma * (1.0 + pre_gate * (1.0 - sigma))).astype(BF)
    grad_up = (grad_act * silu_val).astype(BF)

    def quarter_of(step):
        at = ((y + step) % NY) * quarter
        part = dot_t(grad_gate, lax.dynamic_slice_in_dim(wgate, at, quarter, 0))
        return part + dot_t(grad_up, lax.dynamic_slice_in_dim(wup, at, quarter, 0))

    far = quarter_of(2).astype(BF)
    far_up, far_down = move_y(far[:, :eighth], 1), move_y(far[:, eighth:], -1)
    up, down, mine = quarter_of(1), quarter_of(-1), quarter_of(0)
    up = jnp.concatenate([up[:, :eighth] + far_up, up[:, eighth:]], axis=1).astype(BF)
    down = jnp.concatenate([down[:, :eighth], down[:, eighth:] + far_down], axis=1).astype(BF)
    share = (mine + move_y(up, 1).astype(F32) + move_y(down, -1).astype(F32)).astype(BF)

    extra = jnp.concatenate([slot_gate, jnp.zeros((slot_gate.shape[0], 127), BF)], axis=1)
    back = back_x(jnp.concatenate([share, extra], axis=1))
    partial = lax.dot_general(
        picker, back[:, :quarter], (((0,), (0,)), ((), ())), preferred_element_type=F32
    ).astype(BF)
    gate_back = back[:, quarter : quarter + 1].astype(F32).reshape(8, NZ * CAP, 1)
    by_expert = jnp.sum(jnp.where(picked, gate_back, 0.0), axis=1).T
    gate_tok = jnp.sum(jnp.where(hit, by_expert[:, :, None], 0.0), axis=1).astype(BF)
    partial = jnp.concatenate([partial, gate_tok, jnp.zeros((count, 120), BF)], axis=1)
    total = jnp.zeros((rows, quarter + 128), F32)
    for i, dz in enumerate(ZS):
        total = total + move(partial[i * rows : (i + 1) * rows], dz=-dz).astype(F32)
    return (total[:, :quarter].astype(BF), total[:, quarter : quarter + 8].astype(BF))


def solution(mesh):
    return jax.shard_map(
        on_device,
        mesh=mesh,
        in_specs=(
            P("expert", None),
            P("expert", None),
            P("expert", None),
            P("expert", None),
            P("expert", None, "etp"),
            P("expert", None, "etp"),
            P("expert", "etp", None),
        ),
        out_specs=(P("expert", "etp"), P("expert", None)),
        check_vma=False,
    )
```

```python
import functools

import jax
import jax.numpy as jnp
from jax import lax
from jax.experimental import pallas as pl
from jax.experimental.pallas import tpu as pltpu
from jax.sharding import PartitionSpec as P

BF = jnp.bfloat16
F32 = jnp.float32
NX, NZ, NC, NY = 4, 8, 2, 4
CAP = 5
XS = (0, 1, -1, 2)
SHIFTS = tuple((dx, dc) for dx in XS for dc in (0, 1))
ZS = (0, 1, -1, 2, -2, 3, -3, 4)
BLOCK = NZ * CAP
VMEM = pl.BlockSpec(memory_space=pltpu.VMEM)


def params(mib):
    return pltpu.CompilerParams(vmem_limit_bytes=mib << 20)


def after(value, *others):
    return lax.optimization_barrier((value,) + others)[0]


def move(value, dx=0, dz=0, dc=0):
    if dx % NX == 0 and dz % NZ == 0 and dc % NC == 0:
        return value
    pairs = []
    for x in range(NX):
        for z in range(NZ):
            for c in range(NC):
                to = (((x + dx) % NX) * NZ + (z + dz) % NZ) * NC + (c + dc) % NC
                pairs.append(((x * NZ + z) * NC + c, to))
    return lax.ppermute(value, "expert", pairs)


def move_y(value, dy):
    return lax.ppermute(value, "etp", [(y, (y + dy) % NY) for y in range(NY)])


def prepare_kernel(at_ref, tok_ref, grad_ref, routes_ref, gates_ref, first_out, second_out):
    width = tok_ref.shape[1]
    half, quarter = width // 2, width // 4
    rows = tok_ref.shape[0]
    start = quarter + 128
    more = first_out.shape[1] - start

    def put(i):
        first_out[:, :quarter] = tok_ref[:, i * quarter : (i + 1) * quarter]
        at = i % 2 * half
        first_out[:, start:] = grad_ref[:, at : at + more]
        second_out[...] = grad_ref[:, at + more : at + half]

    for i in range(NY):
        pl.when(at_ref[0] == i)(functools.partial(put, i))
    meta = [routes_ref[...].astype(F32), gates_ref[...].astype(F32), jnp.zeros((rows, 112), F32)]
    first_out[:, quarter:start] = jnp.concatenate(meta, axis=1).astype(BF)


def prepare(y, tokens, out_grad, routes, gates):
    rows, width = tokens.shape
    whole = width // 4 + 128 + width // 2
    first = max(whole // 256 * 128, width // 4 + 128)
    return pl.pallas_call(
        prepare_kernel,
        out_shape=[jax.ShapeDtypeStruct((rows, size), BF) for size in (first, whole - first)],
        in_specs=[pl.BlockSpec(memory_space=pltpu.SMEM)] + [VMEM] * 4,
        out_specs=[VMEM] * 2,
        compiler_params=params(8),
    )(y.reshape(1), tokens, out_grad, routes, gates)


def select_kernel(tile, pieces, picker_ref, *refs):
    count = len(pieces) * NZ
    outs = refs[count:]
    rows = outs[0].shape[0]
    target = 0
    for n, (first, last) in enumerate(pieces):
        blocks = refs[n * NZ : (n + 1) * NZ]

        def step(start, size, blocks=blocks, shift=target - first):
            part = jnp.concatenate([ref[:, pl.ds(start, size)] for ref in blocks], axis=0)
            found = jnp.dot(picker_ref[...], part, preferred_element_type=F32)
            for i, ref in enumerate(outs):
                ref[:, pl.ds(start + shift, size)] = found[i * rows : (i + 1) * rows].astype(BF)

        def body(i, carry, step=step, first=first):
            step(pl.multiple_of(first + i * tile, 128), tile)
            return carry

        lax.fori_loop(0, (last - first) // tile, body, 0)
        rest = (last - first) % tile
        if rest:
            step(last - rest, rest)
        target += last - first


def select(picker, pieces, count):
    rows = picker.shape[0] // count
    spans = tuple((first, last) for _, first, last in pieces)
    width = sum(last - first for first, last in spans)
    blocks = sum([blocks for blocks, _, _ in pieces], [])
    return pl.pallas_call(
        functools.partial(select_kernel, 512, spans),
        out_shape=[jax.ShapeDtypeStruct((rows, width), BF)] * count,
        in_specs=[VMEM] * (1 + len(blocks)),
        out_specs=[VMEM] * count,
        compiler_params=params(16),
        cost_estimate=pl.CostEstimate(
            flops=2 * picker.size * width, bytes_accessed=NZ * 104 * width * 2, transcendentals=0
        ),
    )(picker, *blocks)


def combine_kernel(tile, picker_ref, gate_ref, *refs):
    blocks, outs = refs[: len(SHIFTS)], refs[len(SHIFTS) :]
    width = blocks[0].shape[1]
    rows = outs[0].shape[0]

    def body(i, carry):
        columns = pl.ds(pl.multiple_of(i * tile, tile), tile)
        part = jnp.concatenate([ref[:, columns].astype(F32) for ref in blocks], axis=0).astype(BF)
        found = lax.dot_general(
            picker_ref[...], part, (((0,), (0,)), ((), ())), preferred_element_type=F32
        )
        for b, ref in enumerate(outs):
            ref[:, columns] = found[b * rows : (b + 1) * rows].astype(BF)
        return carry

    lax.fori_loop(0, (width - 128) // tile, body, 0)
    for b, ref in enumerate(outs):
        ref[:, width - 128 :] = gate_ref[b * rows : (b + 1) * rows]


def combine(picker, gate_tok, blocks):
    width = blocks[0].shape[1]
    rows = picker.shape[1] // NZ
    tile = 256 if (width - 128) % 256 == 0 else 128
    return pl.pallas_call(
        functools.partial(combine_kernel, tile),
        out_shape=[jax.ShapeDtypeStruct((rows, width), BF)] * NZ,
        in_specs=[VMEM] * (2 + len(SHIFTS)),
        out_specs=[VMEM] * NZ,
        compiler_params=params(16),
        cost_estimate=pl.CostEstimate(
            flops=2 * picker.size * width, bytes_accessed=NZ * 72 * width * 2, transcendentals=0
        ),
    )(picker, gate_tok, *blocks)


def dot(a, b):
    return jnp.dot(a, b, preferred_element_type=F32)


def dot_t(a, b):
    return lax.dot_general(a, b, (((1,), (1,)), ((), ())), preferred_element_type=F32)


def backward_kernel(*refs):
    gate_ref, up_ref, raw_ref, scale_ref, low_ref, high_ref = refs[:6]
    wd_low, wd_high, wg_far, wu_far = refs[6:10]
    gg_out, gu_out, own_out, far_up, far_down = refs[10:]
    eighth = far_up.shape[1] - 128
    pre_gate, pre_up = gate_ref[...], up_ref[...]
    raw = raw_ref[...] + dot_t(low_ref[...], wd_low[...]) + dot_t(high_ref[...], wd_high[...])
    sigma = jax.nn.sigmoid(pre_gate)
    silu_val = pre_gate * sigma
    act = (silu_val * pre_up).astype(BF)
    rest = jnp.sum(act.astype(F32) * raw, axis=1, keepdims=True)
    grad_act = raw * scale_ref[...]
    grad_gate = (grad_act * pre_up * sigma * (1.0 + pre_gate * (1.0 - sigma))).astype(BF)
    grad_up = (grad_act * silu_val).astype(BF)
    gg_out[...] = grad_gate
    gu_out[...] = grad_up
    lane = lax.broadcasted_iota(jnp.int32, own_out.shape, 1)
    columns = jnp.zeros(own_out.shape, F32)
    for i in range(3):
        piece = rest.astype(BF).astype(F32)
        columns = jnp.where(lane == i, piece, columns)
        rest = rest - piece
    columns = columns.astype(BF)
    own_out[...] = columns
    for out, at in ((far_up, 0), (far_down, eighth)):
        rows = slice(at, at + eighth)
        far = dot_t(grad_gate, wg_far[rows, :]) + dot_t(grad_up, wu_far[rows, :])
        out[:, :eighth] = far.astype(BF)
        out[:, eighth:] = columns


def backward(*args):
    rows, hidden = args[0].shape
    eighth = args[4].shape[1] // 2
    shape = jax.ShapeDtypeStruct
    return pl.pallas_call(
        backward_kernel,
        out_shape=(
            [shape((rows, hidden), BF)] * 2
            + [shape((rows, 128), BF)]
            + [shape((rows, eighth + 128), BF)] * 2
        ),
        in_specs=[VMEM] * len(args),
        out_specs=[VMEM] * 5,
        compiler_params=params(32),
    )(*args)


def neighbours_kernel(gg_ref, gu_ref, wg_up, wu_up, wg_down, wu_down, *outs):
    up_low, up_high, down_low, down_high = outs
    eighth = up_low.shape[1]
    gg, gu = gg_ref[...], gu_ref[...]
    for wg, wu, low, high in ((wg_up, wu_up, up_low, up_high), (wg_down, wu_down, down_low, down_high)):
        for out, at in ((low, 0), (high, eighth)):
            rows = slice(at, at + eighth)
            out[...] = (dot_t(gg, wg[rows, :]) + dot_t(gu, wu[rows, :])).astype(out.dtype)


def neighbours(*args):
    rows, eighth = args[0].shape[0], args[2].shape[0] // 2
    kinds = (F32, BF, BF, F32)
    return pl.pallas_call(
        neighbours_kernel,
        out_shape=[jax.ShapeDtypeStruct((rows, eighth), kind) for kind in kinds],
        in_specs=[VMEM] * len(args),
        out_specs=[VMEM] * 4,
        compiler_params=params(32),
    )(*args)


def forward_kernel(up_low, up_high, down_low, down_high, far_up, far_down, up, down):
    eighth = up_low.shape[1]
    up[:, :eighth] = (up_low[...] + far_up[:, :eighth].astype(F32)).astype(BF)
    up[:, eighth : 2 * eighth] = up_high[...]
    up[:, 2 * eighth :] = far_up[:, eighth:]
    down[:, :eighth] = down_low[...]
    down[:, eighth:] = (down_high[...] + far_down[:, :eighth].astype(F32)).astype(BF)


def forward(*args):
    rows, eighth = args[0].shape
    return pl.pallas_call(
        forward_kernel,
        out_shape=[jax.ShapeDtypeStruct((rows, 2 * eighth + more), BF) for more in (128, 0)],
        in_specs=[VMEM] * len(args),
        out_specs=[VMEM] * 2,
        compiler_params=params(32),
    )(*args)


def finish_kernel(mine, up, down, own, far_up, far_down, *outs):
    quarter = mine.shape[1]
    gate = [
        jnp.sum(ref[:, ref.shape[1] - 128 :].astype(F32), axis=1, keepdims=True)
        for ref in (own, up, far_up, far_down)
    ]
    slot_gate = (gate[0] + gate[1]) + (gate[2] + gate[3])
    lane = lax.broadcasted_iota(jnp.int32, own.shape, 1)
    extra = jnp.where(lane == 0, slot_gate, 0.0)
    for at in range(0, quarter, 128):
        columns = slice(at, at + 128)
        total = mine[:, columns] + up[:, columns].astype(F32) + down[:, columns].astype(F32)
        for i, ref in enumerate(outs):
            ref[:, columns] = total[i * BLOCK : (i + 1) * BLOCK].astype(BF)
    for i, ref in enumerate(outs):
        ref[:, quarter:] = extra[i * BLOCK : (i + 1) * BLOCK].astype(BF)


def finish(mine, *args):
    return pl.pallas_call(
        finish_kernel,
        out_shape=[jax.ShapeDtypeStruct((BLOCK, mine.shape[1] + 128), BF)] * len(SHIFTS),
        in_specs=[VMEM] * (1 + len(args)),
        out_specs=[VMEM] * len(SHIFTS),
        compiler_params=params(32),
    )(mine, *args)


def gather_z(first, second):
    rings = [({0: value}, value, value) for value in (first, second)]
    for step in range(1, 5):
        for n, (blocks, up, down) in enumerate(rings):
            if step < 4 or n == 0:
                up = blocks[step] = move(up, dz=1)
            if step < 4 or n == 1:
                down = move(down, dz=-1)
                blocks[-step if step < 4 else step] = down
            rings[n] = (blocks, up, down)
    return [[blocks[d] for d in ZS] for blocks, _, _ in rings]


def on_device(tokens, out_grad, routes, gates, w_gate, w_up, w_down):
    rows, width = tokens.shape
    half, quarter, eighth = width // 2, width // 4, width // 8
    me = lax.axis_index("expert")
    y = lax.axis_index("etp")
    x, z, core = me // (NZ * NC), (me // NC) % NZ, me % NC
    side = y % 2
    wgate, wup, wdown = w_gate[0], w_up[0], w_down[0]

    first, second = prepare(y, tokens, out_grad, routes, gates)
    meta_end = quarter + 128
    first_z, second_z = gather_z(first, second)

    route_z = jnp.concatenate([b[:, quarter : quarter + 8] for b in first_z], axis=0).astype(F32)
    ids = jnp.stack(
        [((x + dx) % NX) * (NZ * NC) + z * NC + (core + dc) % NC for dx, dc in SHIFTS]
    ).astype(F32)
    hit = route_z[:, None, :] == ids[None, :, None]
    chosen = jnp.any(hit, axis=2).astype(F32)
    count = NZ * rows
    spot = jnp.arange(count, dtype=jnp.int32)
    before = ((spot[:, None] // rows == spot[None, :] // rows) & (spot[:, None] > spot[None, :])).astype(BF)
    position = dot(before, chosen.astype(BF))
    place = jnp.where(chosen > 0, position, -1.0).T
    slot = jnp.arange(BLOCK, dtype=jnp.int32)
    wanted = jnp.where(
        slot[:, None] // CAP == spot[None, :] // rows, (slot[:, None] % CAP).astype(F32), -2.0
    )
    picked = place[:, None, :] == wanted[None, :, :]
    picker = picked.astype(BF).reshape(len(SHIFTS) * BLOCK, count)

    def send_x_twice(parts):
        parts = [move(part, dx=dx) for part, dx in zip(parts, XS)]
        other = [part[BLOCK:] for part in parts]
        near = move(jnp.concatenate(other[1:3], axis=0), dc=1)
        other = [move(other[0], dc=1), near[:BLOCK], near[BLOCK:], move(other[3], dc=1)]
        pairs = [[part[:BLOCK], rest] for part, rest in zip(parts, other)]
        return jnp.concatenate(sum(pairs, []), axis=0)

    tok_rows = select(picker, [(first_z, 0, meta_end)], len(SHIFTS))
    tok_rows = [move(part, dx=dx, dc=dc) for part, (dx, dc) in zip(tok_rows, SHIFTS)]
    tok_x = jnp.concatenate(tok_rows, axis=0)
    tok_own, meta_x = tok_x[:, :quarter], tok_x[:, quarter : quarter + 16].astype(F32)
    tok_up, tok_down = move_y(tok_own, 1), move_y(tok_own, -1)
    tok_far_low, tok_far_high = move_y(tok_up[:, :eighth], 1), move_y(tok_down[:, eighth:], -1)
    pieces = [(first_z, meta_end, first.shape[1]), (second_z, 0, second.shape[1])]
    grad_rows = select(picker, [piece for piece in pieces if piece[1] < piece[2]], len(XS))
    gates_x = (tok_x, tok_rows[2], tok_rows[4], tok_x)
    grad_x = send_x_twice([after(part, gate) for part, gate in zip(grad_rows, gates_x)])
    grad_x = after(grad_x, tok_far_low, tok_far_high)
    grad_low, grad_high = move_y(grad_x[:, :quarter], 1), move_y(grad_x[:, quarter:], -1)
    gate_vals = jnp.sum(
        jnp.where(meta_x[:, :8] == me.astype(F32), meta_x[:, 8:], 0.0), axis=1, keepdims=True
    )
    own_at, low_at = side * half, (1 - side) * half
    high_at = low_at + quarter
    far_at = ((y + 2) % NY) * quarter
    token_parts = (
        (tok_own, y * quarter),
        (tok_up, ((y - 1) % NY) * quarter),
        (tok_down, ((y + 1) % NY) * quarter),
        (tok_far_low, far_at),
        (tok_far_high, far_at + eighth),
    )

    def by_rows(weight):
        return sum(
            dot(part, lax.dynamic_slice_in_dim(weight, at, part.shape[1], 0))
            for part, at in token_parts
        )

    pre_gate = by_rows(wgate)
    pre_up = by_rows(wup)
    raw = dot_t(grad_x, lax.dynamic_slice_in_dim(wdown, own_at, half, 1))
    wgate, wup, wdown = [after(w, tok_up) for w in (wgate, wup, wdown)]
    wd_low, wd_high = [
        lax.dynamic_slice_in_dim(wdown, at, quarter, 1) for at in (low_at, high_at)
    ]

    def quarters(step):
        at = ((y + step) % NY) * quarter
        return [lax.dynamic_slice_in_dim(w, at, quarter, 0) for w in (wgate, wup)]

    grad_gate, grad_up, own_gate, far_up, far_down = backward(
        pre_gate, pre_up, raw, gate_vals, grad_low, grad_high, wd_low, wd_high, *quarters(2)
    )
    far_up, far_down = move_y(far_up, 1), move_y(far_down, -1)
    near = neighbours(grad_gate, grad_up, *quarters(1), *quarters(-1))
    up, down = forward(*near, far_up, far_down)
    up, down = move_y(up, 1), move_y(down, -1)
    mine = sum(dot_t(g, w) for g, w in zip((grad_gate, grad_up), quarters(0)))
    share = finish(mine, up, down, own_gate, far_up, far_down)
    back = [move(part, dx=-dx, dc=-dc) for part, (dx, dc) in zip(share, SHIFTS)]

    gate_back = jnp.stack([b[:, quarter : quarter + 1] for b in back]).astype(F32)
    by_expert = jnp.sum(jnp.where(picked, gate_back, 0.0), axis=1).T
    gate_tok = jnp.sum(jnp.where(hit, by_expert[:, :, None], 0.0), axis=1).astype(BF)
    gate_tok = jnp.concatenate([gate_tok, jnp.zeros((count, 120), BF)], axis=1)
    partial = combine(picker, gate_tok, back)
    total = jnp.zeros((rows, quarter + 128), F32)
    for i, dz in enumerate(ZS):
        total = total + move(partial[i], dz=-dz).astype(F32)
    return (total[:, :quarter].astype(BF), total[:, quarter : quarter + 8].astype(BF))


def solution(mesh):
    return jax.shard_map(
        on_device,
        mesh=mesh,
        in_specs=(
            P("expert", None),
            P("expert", None),
            P("expert", None),
            P("expert", None),
            P("expert", None, "etp"),
            P("expert", None, "etp"),
            P("expert", "etp", None),
        ),
        out_specs=(P("expert", "etp"), P("expert", None)),
        check_vma=False,
    )
```

```python
import functools

import jax
import jax.numpy as jnp
from jax import lax
from jax.experimental import pallas as pl
from jax.experimental.pallas import tpu as pltpu
from jax.sharding import PartitionSpec as P

BF = jnp.bfloat16
F32 = jnp.float32
NX, NZ, NC, NY = 4, 8, 2, 4
CAP = 5
XS = (0, 1, -1, 2)
SHIFTS = tuple((dx, dc) for dx in XS for dc in (0, 1))
ZS = (0, 1, -1, 2, -2, 3, -3, 4)
BLOCK = NZ * CAP
VMEM = pl.BlockSpec(memory_space=pltpu.VMEM)


def params(mib):
    return pltpu.CompilerParams(vmem_limit_bytes=mib << 20)


def after(value, *others):
    return lax.optimization_barrier((value,) + others)[0]


def move(value, dx=0, dz=0, dc=0):
    if dx % NX == 0 and dz % NZ == 0 and dc % NC == 0:
        return value
    pairs = []
    for x in range(NX):
        for z in range(NZ):
            for c in range(NC):
                to = (((x + dx) % NX) * NZ + (z + dz) % NZ) * NC + (c + dc) % NC
                pairs.append(((x * NZ + z) * NC + c, to))
    return lax.ppermute(value, "expert", pairs)


def move_y(value, dy):
    return lax.ppermute(value, "etp", [(y, (y + dy) % NY) for y in range(NY)])


def prepare_kernel(at_ref, tok_ref, grad_ref, routes_ref, gates_ref, first_out, second_out, sems):
    half = tok_ref.shape[1] // 2
    quarter = half // 2
    start = quarter + 128
    more = first_out.shape[1] - start
    tok_at = pl.multiple_of(at_ref[0] * quarter, 128)
    grad_at = pl.multiple_of(lax.rem(at_ref[0], 2) * half, 128)
    copies = [
        (tok_ref.at[:, pl.ds(tok_at, quarter)], first_out.at[:, :quarter]),
        (grad_ref.at[:, pl.ds(grad_at + more, half - more)], second_out),
    ]
    if more:
        copies.append((grad_ref.at[:, pl.ds(grad_at, more)], first_out.at[:, start:]))
    copies = [pltpu.make_async_copy(*pair, sems.at[i]) for i, pair in enumerate(copies)]
    for copy in copies:
        copy.start()
    meta = jnp.concatenate([routes_ref[...].astype(F32), gates_ref[...].astype(F32)], axis=0)
    shape = (meta.shape[0], 128)
    unit = lax.broadcasted_iota(jnp.int32, shape, 0) == lax.broadcasted_iota(jnp.int32, shape, 1)
    meta = lax.dot_general(
        meta.astype(BF), unit.astype(BF), (((0,), (0,)), ((), ())), preferred_element_type=F32
    )
    first_out[:, quarter:start] = meta.astype(BF)
    for copy in copies:
        copy.wait()


def prepare(y, tokens, out_grad, routes, gates):
    rows, width = tokens.shape
    whole = width // 4 + 128 + width // 2
    first = max(whole // 256 * 128, width // 4 + 128)
    anywhere = pl.BlockSpec(memory_space=pl.ANY)
    return pl.pallas_call(
        prepare_kernel,
        out_shape=[jax.ShapeDtypeStruct((rows, size), BF) for size in (first, whole - first)],
        in_specs=[pl.BlockSpec(memory_space=pltpu.SMEM), anywhere, anywhere, VMEM, VMEM],
        out_specs=[VMEM] * 2,
        scratch_shapes=[pltpu.SemaphoreType.DMA((3,))],
        compiler_params=params(56),
    )(y.reshape(1), tokens, out_grad, routes.T, gates.T)


def total_kernel(*refs):
    blocks, (grad_out, gate_out) = refs[:NZ], refs[NZ:]
    width = grad_out.shape[1]
    total = blocks[0][...].astype(F32)
    for ref in blocks[1:]:
        total += ref[...].astype(F32)
    grad_out[...] = total[:, :width].astype(BF)
    gate_out[...] = total[:, width : width + gate_out.shape[1]].astype(BF)


def total_of(blocks, choices):
    rows, width = blocks[0].shape
    return pl.pallas_call(
        total_kernel,
        out_shape=[jax.ShapeDtypeStruct((rows, size), BF) for size in (width - 128, choices)],
        in_specs=[VMEM] * NZ,
        out_specs=[VMEM] * 2,
        compiler_params=params(8),
    )(*blocks)


def select_kernel(tile, pieces, picker_ref, *refs):
    count = len(pieces) * NZ
    outs = refs[count:]
    rows = outs[0].shape[0]
    target = 0
    for n, (first, last) in enumerate(pieces):
        blocks = refs[n * NZ : (n + 1) * NZ]

        def step(start, size, blocks=blocks, shift=target - first):
            part = jnp.concatenate([ref[:, pl.ds(start, size)] for ref in blocks], axis=0)
            found = jnp.dot(picker_ref[...], part, preferred_element_type=F32)
            for i, ref in enumerate(outs):
                ref[:, pl.ds(start + shift, size)] = found[i * rows : (i + 1) * rows].astype(BF)

        def body(i, carry, step=step, first=first):
            step(pl.multiple_of(first + i * tile, 128), tile)
            return carry

        lax.fori_loop(0, (last - first) // tile, body, 0)
        rest = (last - first) % tile
        if rest:
            step(last - rest, rest)
        target += last - first


def select(picker, pieces, count):
    rows = picker.shape[0] // count
    spans = tuple((first, last) for _, first, last in pieces)
    width = sum(last - first for first, last in spans)
    blocks = sum([blocks for blocks, _, _ in pieces], [])
    return pl.pallas_call(
        functools.partial(select_kernel, 512, spans),
        out_shape=[jax.ShapeDtypeStruct((rows, width), BF)] * count,
        in_specs=[VMEM] * (1 + len(blocks)),
        out_specs=[VMEM] * count,
        compiler_params=params(16),
        cost_estimate=pl.CostEstimate(
            flops=2 * picker.size * width, bytes_accessed=NZ * 104 * width * 2, transcendentals=0
        ),
    )(picker, *blocks)


def combine_kernel(tile, picker_ref, gate_ref, *refs):
    blocks, outs = refs[: len(SHIFTS)], refs[len(SHIFTS) :]
    width = blocks[0].shape[1]
    rows = outs[0].shape[0]

    def body(i, carry):
        columns = pl.ds(pl.multiple_of(i * tile, tile), tile)
        part = jnp.concatenate([ref[:, columns].astype(F32) for ref in blocks], axis=0).astype(BF)
        found = lax.dot_general(
            picker_ref[...], part, (((0,), (0,)), ((), ())), preferred_element_type=F32
        )
        for b, ref in enumerate(outs):
            ref[:, columns] = found[b * rows : (b + 1) * rows].astype(BF)
        return carry

    lax.fori_loop(0, (width - 128) // tile, body, 0)
    for b, ref in enumerate(outs):
        ref[:, width - 128 :] = gate_ref[b * rows : (b + 1) * rows]


def combine(picker, gate_tok, blocks):
    width = blocks[0].shape[1]
    rows = picker.shape[1] // NZ
    tile = 256 if (width - 128) % 256 == 0 else 128
    return pl.pallas_call(
        functools.partial(combine_kernel, tile),
        out_shape=[jax.ShapeDtypeStruct((rows, width), BF)] * NZ,
        in_specs=[VMEM] * (2 + len(SHIFTS)),
        out_specs=[VMEM] * NZ,
        compiler_params=params(16),
        cost_estimate=pl.CostEstimate(
            flops=2 * picker.size * width, bytes_accessed=NZ * 72 * width * 2, transcendentals=0
        ),
    )(picker, gate_tok, *blocks)


def dot(a, b):
    return jnp.dot(a, b, preferred_element_type=F32)


def dot_t(a, b):
    return lax.dot_general(a, b, (((1,), (1,)), ((), ())), preferred_element_type=F32)


def backward_kernel(*refs):
    gate_ref, up_ref, raw_ref, scale_ref, low_ref, high_ref = refs[:6]
    wd_low, wd_high, wg_far, wu_far = refs[6:10]
    gg_out, gu_out, own_out, far_up, far_down = refs[10:]
    eighth = far_up.shape[1] - 128
    pre_gate, pre_up = gate_ref[...], up_ref[...]
    raw = raw_ref[...] + dot_t(low_ref[...], wd_low[...]) + dot_t(high_ref[...], wd_high[...])
    sigma = jax.nn.sigmoid(pre_gate)
    silu_val = pre_gate * sigma
    act = (silu_val * pre_up).astype(BF)
    rest = jnp.sum(act.astype(F32) * raw, axis=1, keepdims=True)
    grad_act = raw * scale_ref[...]
    grad_gate = (grad_act * pre_up * sigma * (1.0 + pre_gate * (1.0 - sigma))).astype(BF)
    grad_up = (grad_act * silu_val).astype(BF)
    gg_out[...] = grad_gate
    gu_out[...] = grad_up
    lane = lax.broadcasted_iota(jnp.int32, own_out.shape, 1)
    columns = jnp.zeros(own_out.shape, F32)
    for i in range(3):
        piece = rest.astype(BF).astype(F32)
        columns = jnp.where(lane == i, piece, columns)
        rest = rest - piece
    columns = columns.astype(BF)
    own_out[...] = columns
    for out, at in ((far_up, 0), (far_down, eighth)):
        rows = slice(at, at + eighth)
        far = dot_t(grad_gate, wg_far[rows, :]) + dot_t(grad_up, wu_far[rows, :])
        out[:, :eighth] = far.astype(BF)
        out[:, eighth:] = columns


def backward(*args):
    rows, hidden = args[0].shape
    eighth = args[4].shape[1] // 2
    shape = jax.ShapeDtypeStruct
    return pl.pallas_call(
        backward_kernel,
        out_shape=(
            [shape((rows, hidden), BF)] * 2
            + [shape((rows, 128), BF)]
            + [shape((rows, eighth + 128), BF)] * 2
        ),
        in_specs=[VMEM] * len(args),
        out_specs=[VMEM] * 5,
        compiler_params=params(32),
    )(*args)


def neighbours_kernel(gg_ref, gu_ref, wg_up, wu_up, wg_down, wu_down, *outs):
    up_low, up_high, down_low, down_high = outs
    eighth = up_low.shape[1]
    gg, gu = gg_ref[...], gu_ref[...]
    for wg, wu, low, high in ((wg_up, wu_up, up_low, up_high), (wg_down, wu_down, down_low, down_high)):
        for out, at in ((low, 0), (high, eighth)):
            rows = slice(at, at + eighth)
            out[...] = (dot_t(gg, wg[rows, :]) + dot_t(gu, wu[rows, :])).astype(out.dtype)


def neighbours(*args):
    rows, eighth = args[0].shape[0], args[2].shape[0] // 2
    kinds = (F32, BF, BF, F32)
    return pl.pallas_call(
        neighbours_kernel,
        out_shape=[jax.ShapeDtypeStruct((rows, eighth), kind) for kind in kinds],
        in_specs=[VMEM] * len(args),
        out_specs=[VMEM] * 4,
        compiler_params=params(32),
    )(*args)


def forward_kernel(up_low, up_high, down_low, down_high, far_up, far_down, up, down):
    eighth = up_low.shape[1]
    up[:, :eighth] = (up_low[...] + far_up[:, :eighth].astype(F32)).astype(BF)
    up[:, eighth : 2 * eighth] = up_high[...]
    up[:, 2 * eighth :] = far_up[:, eighth:]
    down[:, :eighth] = down_low[...]
    down[:, eighth:] = (down_high[...] + far_down[:, :eighth].astype(F32)).astype(BF)


def forward(*args):
    rows, eighth = args[0].shape
    return pl.pallas_call(
        forward_kernel,
        out_shape=[jax.ShapeDtypeStruct((rows, 2 * eighth + more), BF) for more in (128, 0)],
        in_specs=[VMEM] * len(args),
        out_specs=[VMEM] * 2,
        compiler_params=params(32),
    )(*args)


def finish_kernel(mine, up, down, own, far_up, far_down, *outs):
    quarter = mine.shape[1]
    gate = [
        jnp.sum(ref[:, ref.shape[1] - 128 :].astype(F32), axis=1, keepdims=True)
        for ref in (own, up, far_up, far_down)
    ]
    slot_gate = (gate[0] + gate[1]) + (gate[2] + gate[3])
    lane = lax.broadcasted_iota(jnp.int32, own.shape, 1)
    extra = jnp.where(lane == 0, slot_gate, 0.0)
    for at in range(0, quarter, 128):
        columns = slice(at, at + 128)
        total = mine[:, columns] + up[:, columns].astype(F32) + down[:, columns].astype(F32)
        for i, ref in enumerate(outs):
            ref[:, columns] = total[i * BLOCK : (i + 1) * BLOCK].astype(BF)
    for i, ref in enumerate(outs):
        ref[:, quarter:] = extra[i * BLOCK : (i + 1) * BLOCK].astype(BF)


def finish(mine, *args):
    return pl.pallas_call(
        finish_kernel,
        out_shape=[jax.ShapeDtypeStruct((BLOCK, mine.shape[1] + 128), BF)] * len(SHIFTS),
        in_specs=[VMEM] * (1 + len(args)),
        out_specs=[VMEM] * len(SHIFTS),
        compiler_params=params(32),
    )(mine, *args)


def gather_z(first, second):
    rings = [({0: value}, value, value) for value in (first, second)]
    for step in range(1, 5):
        for n, (blocks, up, down) in enumerate(rings):
            if step < 4 or n == 0:
                up = blocks[step] = move(up, dz=1)
            if step < 4 or n == 1:
                down = move(down, dz=-1)
                blocks[-step if step < 4 else step] = down
            rings[n] = (blocks, up, down)
    return [[blocks[d] for d in ZS] for blocks, _, _ in rings]


def on_device(tokens, out_grad, routes, gates, w_gate, w_up, w_down):
    rows, width = tokens.shape
    half, quarter, eighth = width // 2, width // 4, width // 8
    me = lax.axis_index("expert")
    y = lax.axis_index("etp")
    x, z, core = me // (NZ * NC), (me // NC) % NZ, me % NC
    side = y % 2
    wgate, wup, wdown = w_gate[0], w_up[0], w_down[0]

    first, second = prepare(y, tokens, out_grad, routes, gates)
    meta_end = quarter + 128
    first_z, second_z = gather_z(first, second)

    route_z = jnp.concatenate([b[:, quarter : quarter + 8] for b in first_z], axis=0).astype(F32)
    ids = jnp.stack(
        [((x + dx) % NX) * (NZ * NC) + z * NC + (core + dc) % NC for dx, dc in SHIFTS]
    ).astype(F32)
    hit = route_z[:, None, :] == ids[None, :, None]
    chosen = jnp.any(hit, axis=2).astype(F32)
    count = NZ * rows
    spot = jnp.arange(count, dtype=jnp.int32)
    before = ((spot[:, None] // rows == spot[None, :] // rows) & (spot[:, None] > spot[None, :])).astype(BF)
    position = dot(before, chosen.astype(BF))
    place = jnp.where(chosen > 0, position, -1.0).T
    slot = jnp.arange(BLOCK, dtype=jnp.int32)
    wanted = jnp.where(
        slot[:, None] // CAP == spot[None, :] // rows, (slot[:, None] % CAP).astype(F32), -2.0
    )
    picked = place[:, None, :] == wanted[None, :, :]
    picker = picked.astype(BF).reshape(len(SHIFTS) * BLOCK, count)

    def send_x_twice(parts, early):
        own = move(parts[0][BLOCK:], dc=1)
        near = [move(part, dx=dx) for part, dx in zip(parts[1:3], XS[1:3])]
        far = move(after(parts[3], *near), dx=XS[3])
        parts = [parts[0], *near, far]
        other = [part[BLOCK:] for part in parts]
        near = move(after(jnp.concatenate(other[1:3], axis=0), *early), dc=1)
        other = [own, near[:BLOCK], near[BLOCK:], move(other[3], dc=1)]
        pairs = [[part[:BLOCK], rest] for part, rest in zip(parts, other)]
        return jnp.concatenate(sum(pairs, []), axis=0)

    tok_rows = select(picker, [(first_z, 0, meta_end)], len(SHIFTS))
    tok_rows = [move(part, dx=dx, dc=dc) for part, (dx, dc) in zip(tok_rows, SHIFTS)]
    tok_x = jnp.concatenate(tok_rows, axis=0)
    tok_own, meta_x = tok_x[:, :quarter], tok_x[:, quarter : quarter + 16].astype(F32)
    tok_up, tok_down = move_y(tok_own, 1), move_y(tok_own, -1)
    tok_far_low, tok_far_high = move_y(tok_up[:, :eighth], 1), move_y(tok_down[:, eighth:], -1)
    pieces = [(first_z, meta_end, first.shape[1]), (second_z, 0, second.shape[1])]
    grad_rows = select(picker, [piece for piece in pieces if piece[1] < piece[2]], len(XS))
    gates_x = (tok_x, tok_rows[2], tok_rows[4], tok_x)
    grad_x = send_x_twice([after(part, gate) for part, gate in zip(grad_rows, gates_x)], (tok_up, tok_down))
    grad_low, grad_high = move_y(grad_x[:, :quarter], 1), move_y(grad_x[:, quarter:], -1)
    gate_vals = jnp.sum(
        jnp.where(meta_x[:, :8] == me.astype(F32), meta_x[:, 8:], 0.0), axis=1, keepdims=True
    )
    own_at, low_at = side * half, (1 - side) * half
    high_at = low_at + quarter
    far_at = ((y + 2) % NY) * quarter
    token_parts = (
        (tok_own, y * quarter),
        (tok_up, ((y - 1) % NY) * quarter),
        (tok_down, ((y + 1) % NY) * quarter),
        (tok_far_low, far_at),
        (tok_far_high, far_at + eighth),
    )

    def by_rows(weight):
        return sum(
            dot(part, lax.dynamic_slice_in_dim(weight, at, part.shape[1], 0))
            for part, at in token_parts
        )

    pre_gate = by_rows(wgate)
    pre_up = by_rows(wup)
    raw = dot_t(grad_x, lax.dynamic_slice_in_dim(wdown, own_at, half, 1))
    wgate, wup, wdown = [after(w, tok_up) for w in (wgate, wup, wdown)]
    wd_low, wd_high = [
        lax.dynamic_slice_in_dim(wdown, at, quarter, 1) for at in (low_at, high_at)
    ]

    def quarters(step):
        at = ((y + step) % NY) * quarter
        return [lax.dynamic_slice_in_dim(w, at, quarter, 0) for w in (wgate, wup)]

    grad_gate, grad_up, own_gate, far_up, far_down = backward(
        pre_gate, pre_up, raw, gate_vals, grad_low, grad_high, wd_low, wd_high, *quarters(2)
    )
    far_up, far_down = move_y(far_up, 1), move_y(far_down, -1)
    near = neighbours(grad_gate, grad_up, *quarters(1), *quarters(-1))
    up, down = forward(*near, far_up, far_down)
    up, down = move_y(up, 1), move_y(down, -1)
    mine = sum(dot_t(g, w) for g, w in zip((grad_gate, grad_up), quarters(0)))
    share = finish(mine, up, down, own_gate, far_up, far_down)
    back = [move(part, dx=-dx, dc=-dc) for part, (dx, dc) in zip(share, SHIFTS)]

    gate_back = jnp.stack([b[:, quarter : quarter + 1] for b in back]).astype(F32)
    by_expert = jnp.sum(jnp.where(picked, gate_back, 0.0), axis=1).T
    gate_tok = jnp.sum(jnp.where(hit, by_expert[:, :, None], 0.0), axis=1).astype(BF)
    gate_tok = jnp.concatenate([gate_tok, jnp.zeros((count, 120), BF)], axis=1)
    partial = combine(picker, gate_tok, back)
    arrived = [move(part, dz=-dz) for part, dz in zip(partial, ZS)]
    return tuple(total_of(arrived, routes.shape[1]))


def solution(mesh):
    return jax.shard_map(
        on_device,
        mesh=mesh,
        in_specs=(
            P("expert", None),
            P("expert", None),
            P("expert", None),
            P("expert", None),
            P("expert", None, "etp"),
            P("expert", None, "etp"),
            P("expert", "etp", None),
        ),
        out_specs=(P("expert", "etp"), P("expert", None)),
        check_vma=False,
    )
```

```python
import functools

import jax
import jax.numpy as jnp
from jax import lax
from jax.experimental import pallas as pl
from jax.experimental.pallas import tpu as pltpu
from jax.sharding import PartitionSpec as P

BF = jnp.bfloat16
F32 = jnp.float32
NX, NZ, NC, NY = 4, 8, 2, 4
CAP = 5
XS = (0, 1, -1, 2)
SHIFTS = tuple((dx, dc) for dx in XS for dc in (0, 1))
ZS = (0, 1, -1, 2, -2, 3, -3, 4)
BLOCK = NZ * CAP
VMEM = pl.BlockSpec(memory_space=pltpu.VMEM)


def params(mib):
    return pltpu.CompilerParams(vmem_limit_bytes=mib << 20)


def after(value, *others):
    return lax.optimization_barrier((value,) + others)[0]


def move(value, dx=0, dz=0, dc=0):
    if dx % NX == 0 and dz % NZ == 0 and dc % NC == 0:
        return value
    pairs = []
    for x in range(NX):
        for z in range(NZ):
            for c in range(NC):
                to = (((x + dx) % NX) * NZ + (z + dz) % NZ) * NC + (c + dc) % NC
                pairs.append(((x * NZ + z) * NC + c, to))
    return lax.ppermute(value, "expert", pairs)


def move_y(value, dy):
    return lax.ppermute(value, "etp", [(y, (y + dy) % NY) for y in range(NY)])


def prepare_kernel(at_ref, tok_ref, grad_ref, routes_ref, gates_ref, first_out, second_out, sems):
    half = tok_ref.shape[1] // 2
    quarter = half // 2
    start = quarter + 128
    more = first_out.shape[1] - start
    tok_at = pl.multiple_of(at_ref[0] * quarter, 128)
    grad_at = pl.multiple_of(lax.rem(at_ref[0], 2) * half, 128)
    copies = [
        (tok_ref.at[:, pl.ds(tok_at, quarter)], first_out.at[:, :quarter]),
        (grad_ref.at[:, pl.ds(grad_at + more, half - more)], second_out),
    ]
    if more:
        copies.append((grad_ref.at[:, pl.ds(grad_at, more)], first_out.at[:, start:]))
    copies = [pltpu.make_async_copy(*pair, sems.at[i]) for i, pair in enumerate(copies)]
    for copy in copies:
        copy.start()
    meta = jnp.concatenate([routes_ref[...].astype(F32), gates_ref[...].astype(F32)], axis=0)
    shape = (meta.shape[0], 128)
    unit = lax.broadcasted_iota(jnp.int32, shape, 0) == lax.broadcasted_iota(jnp.int32, shape, 1)
    meta = lax.dot_general(
        meta.astype(BF), unit.astype(BF), (((0,), (0,)), ((), ())), preferred_element_type=F32
    )
    first_out[:, quarter:start] = meta.astype(BF)
    for copy in copies:
        copy.wait()


def prepare(y, tokens, out_grad, routes, gates):
    rows, width = tokens.shape
    whole = width // 4 + 128 + width // 2
    first = max(whole // 256 * 128, width // 4 + 128)
    anywhere = pl.BlockSpec(memory_space=pl.ANY)
    return pl.pallas_call(
        prepare_kernel,
        out_shape=[jax.ShapeDtypeStruct((rows, size), BF) for size in (first, whole - first)],
        in_specs=[pl.BlockSpec(memory_space=pltpu.SMEM), anywhere, anywhere, VMEM, VMEM],
        out_specs=[VMEM] * 2,
        scratch_shapes=[pltpu.SemaphoreType.DMA((3,))],
        compiler_params=params(56),
    )(y.reshape(1), tokens, out_grad, routes.T, gates.T)


def total_kernel(*refs):
    blocks, (grad_out, gate_out) = refs[:NZ], refs[NZ:]
    width = grad_out.shape[1]
    total = blocks[0][...].astype(F32)
    for ref in blocks[1:]:
        total += ref[...].astype(F32)
    grad_out[...] = total[:, :width].astype(BF)
    gate_out[...] = total[:, width : width + gate_out.shape[1]].astype(BF)


def total_of(blocks, choices):
    rows, width = blocks[0].shape
    return pl.pallas_call(
        total_kernel,
        out_shape=[jax.ShapeDtypeStruct((rows, size), BF) for size in (width - 128, choices)],
        in_specs=[VMEM] * NZ,
        out_specs=[VMEM] * 2,
        compiler_params=params(8),
    )(*blocks)


def select_kernel(tile, pieces, picker_ref, *refs):
    count = len(pieces) * NZ
    outs = refs[count:]
    rows = outs[0].shape[0]
    target = 0
    for n, (first, last) in enumerate(pieces):
        blocks = refs[n * NZ : (n + 1) * NZ]

        def step(start, size, blocks=blocks, shift=target - first):
            part = jnp.concatenate([ref[:, pl.ds(start, size)] for ref in blocks], axis=0)
            found = jnp.dot(picker_ref[...], part, preferred_element_type=F32)
            for i, ref in enumerate(outs):
                ref[:, pl.ds(start + shift, size)] = found[i * rows : (i + 1) * rows].astype(BF)

        def body(i, carry, step=step, first=first):
            step(pl.multiple_of(first + i * tile, 128), tile)
            return carry

        lax.fori_loop(0, (last - first) // tile, body, 0)
        rest = (last - first) % tile
        if rest:
            step(last - rest, rest)
        target += last - first


def select(picker, pieces, count):
    rows = picker.shape[0] // count
    spans = tuple((first, last) for _, first, last in pieces)
    width = sum(last - first for first, last in spans)
    blocks = sum([blocks for blocks, _, _ in pieces], [])
    return pl.pallas_call(
        functools.partial(select_kernel, 512, spans),
        out_shape=[jax.ShapeDtypeStruct((rows, width), BF)] * count,
        in_specs=[VMEM] * (1 + len(blocks)),
        out_specs=[VMEM] * count,
        compiler_params=params(16),
        cost_estimate=pl.CostEstimate(
            flops=2 * picker.size * width, bytes_accessed=NZ * 104 * width * 2, transcendentals=0
        ),
    )(picker, *blocks)


def combine_kernel(tile, picker_ref, gate_ref, *refs):
    blocks, outs = refs[: len(SHIFTS)], refs[len(SHIFTS) :]
    width = blocks[0].shape[1]
    rows = outs[0].shape[0]

    def body(i, carry):
        columns = pl.ds(pl.multiple_of(i * tile, tile), tile)
        part = jnp.concatenate([ref[:, columns].astype(F32) for ref in blocks], axis=0).astype(BF)
        found = lax.dot_general(
            picker_ref[...], part, (((0,), (0,)), ((), ())), preferred_element_type=F32
        )
        for b, ref in enumerate(outs):
            ref[:, columns] = found[b * rows : (b + 1) * rows].astype(BF)
        return carry

    lax.fori_loop(0, (width - 128) // tile, body, 0)
    for b, ref in enumerate(outs):
        ref[:, width - 128 :] = gate_ref[b * rows : (b + 1) * rows]


def combine(picker, gate_tok, blocks):
    width = blocks[0].shape[1]
    rows = picker.shape[1] // NZ
    tile = 256 if (width - 128) % 256 == 0 else 128
    return pl.pallas_call(
        functools.partial(combine_kernel, tile),
        out_shape=[jax.ShapeDtypeStruct((rows, width), BF)] * NZ,
        in_specs=[VMEM] * (2 + len(SHIFTS)),
        out_specs=[VMEM] * NZ,
        compiler_params=params(16),
        cost_estimate=pl.CostEstimate(
            flops=2 * picker.size * width, bytes_accessed=NZ * 72 * width * 2, transcendentals=0
        ),
    )(picker, gate_tok, *blocks)


def dot(a, b):
    return jnp.dot(a, b, preferred_element_type=F32)


def dot_t(a, b):
    return lax.dot_general(a, b, (((1,), (1,)), ((), ())), preferred_element_type=F32)


def backward_kernel(*refs):
    gate_ref, up_ref, raw_ref, scale_ref, low_ref, high_ref = refs[:6]
    wd_low, wd_high, wg_far, wu_far = refs[6:10]
    gg_out, gu_out, own_out, far_up, far_down = refs[10:]
    eighth = far_up.shape[1] - 128
    pre_gate, pre_up = gate_ref[...], up_ref[...]
    raw = raw_ref[...] + dot_t(low_ref[...], wd_low[...]) + dot_t(high_ref[...], wd_high[...])
    sigma = jax.nn.sigmoid(pre_gate)
    silu_val = pre_gate * sigma
    act = (silu_val * pre_up).astype(BF)
    rest = jnp.sum(act.astype(F32) * raw, axis=1, keepdims=True)
    grad_act = raw * scale_ref[...]
    grad_gate = (grad_act * pre_up * sigma * (1.0 + pre_gate * (1.0 - sigma))).astype(BF)
    grad_up = (grad_act * silu_val).astype(BF)
    gg_out[...] = grad_gate
    gu_out[...] = grad_up
    lane = lax.broadcasted_iota(jnp.int32, own_out.shape, 1)
    columns = jnp.zeros(own_out.shape, F32)
    for i in range(3):
        piece = rest.astype(BF).astype(F32)
        columns = jnp.where(lane == i, piece, columns)
        rest = rest - piece
    columns = columns.astype(BF)
    own_out[...] = columns
    for out, at in ((far_up, 0), (far_down, eighth)):
        rows = slice(at, at + eighth)
        far = dot_t(grad_gate, wg_far[rows, :]) + dot_t(grad_up, wu_far[rows, :])
        out[:, :eighth] = far.astype(BF)
        out[:, eighth:] = columns


def backward(*args):
    rows, hidden = args[0].shape
    eighth = args[4].shape[1] // 2
    shape = jax.ShapeDtypeStruct
    return pl.pallas_call(
        backward_kernel,
        out_shape=(
            [shape((rows, hidden), BF)] * 2
            + [shape((rows, 128), BF)]
            + [shape((rows, eighth + 128), BF)] * 2
        ),
        in_specs=[VMEM] * len(args),
        out_specs=[VMEM] * 5,
        compiler_params=params(32),
    )(*args)


def neighbours_kernel(gg_ref, gu_ref, wg_up, wu_up, wg_down, wu_down, *outs):
    up_low, up_high, down_low, down_high = outs
    eighth = up_low.shape[1]
    gg, gu = gg_ref[...], gu_ref[...]
    for wg, wu, low, high in ((wg_up, wu_up, up_low, up_high), (wg_down, wu_down, down_low, down_high)):
        for out, at in ((low, 0), (high, eighth)):
            rows = slice(at, at + eighth)
            out[...] = (dot_t(gg, wg[rows, :]) + dot_t(gu, wu[rows, :])).astype(out.dtype)


def neighbours(*args):
    rows, eighth = args[0].shape[0], args[2].shape[0] // 2
    kinds = (F32, BF, BF, F32)
    return pl.pallas_call(
        neighbours_kernel,
        out_shape=[jax.ShapeDtypeStruct((rows, eighth), kind) for kind in kinds],
        in_specs=[VMEM] * len(args),
        out_specs=[VMEM] * 4,
        compiler_params=params(32),
    )(*args)


def forward_kernel(up_low, up_high, down_low, down_high, far_up, far_down, up, down):
    eighth = up_low.shape[1]
    up[:, :eighth] = (up_low[...] + far_up[:, :eighth].astype(F32)).astype(BF)
    up[:, eighth : 2 * eighth] = up_high[...]
    up[:, 2 * eighth :] = far_up[:, eighth:]
    down[:, :eighth] = down_low[...]
    down[:, eighth:] = (down_high[...] + far_down[:, :eighth].astype(F32)).astype(BF)


def forward(*args):
    rows, eighth = args[0].shape
    return pl.pallas_call(
        forward_kernel,
        out_shape=[jax.ShapeDtypeStruct((rows, 2 * eighth + more), BF) for more in (128, 0)],
        in_specs=[VMEM] * len(args),
        out_specs=[VMEM] * 2,
        compiler_params=params(32),
    )(*args)


def finish_kernel(mine, up, down, own, far_up, far_down, *outs):
    quarter = mine.shape[1]
    gate = [
        jnp.sum(ref[:, ref.shape[1] - 128 :].astype(F32), axis=1, keepdims=True)
        for ref in (own, up, far_up, far_down)
    ]
    slot_gate = (gate[0] + gate[1]) + (gate[2] + gate[3])
    lane = lax.broadcasted_iota(jnp.int32, own.shape, 1)
    extra = jnp.where(lane == 0, slot_gate, 0.0)
    for at in range(0, quarter, 128):
        columns = slice(at, at + 128)
        total = mine[:, columns] + up[:, columns].astype(F32) + down[:, columns].astype(F32)
        for i, ref in enumerate(outs):
            ref[:, columns] = total[i * BLOCK : (i + 1) * BLOCK].astype(BF)
    for i, ref in enumerate(outs):
        ref[:, quarter:] = extra[i * BLOCK : (i + 1) * BLOCK].astype(BF)


def finish(mine, *args):
    return pl.pallas_call(
        finish_kernel,
        out_shape=[jax.ShapeDtypeStruct((BLOCK, mine.shape[1] + 128), BF)] * len(SHIFTS),
        in_specs=[VMEM] * (1 + len(args)),
        out_specs=[VMEM] * len(SHIFTS),
        compiler_params=params(32),
    )(mine, *args)


def gather_z(first, second):
    rings = [({0: value}, value, value) for value in (first, second)]
    for step in range(1, 5):
        for n, (blocks, up, down) in enumerate(rings):
            if step < 4 or n == 0:
                up = blocks[step] = move(up, dz=1)
            if step < 4 or n == 1:
                down = move(down, dz=-1)
                blocks[-step if step < 4 else step] = down
            rings[n] = (blocks, up, down)
    return [[blocks[d] for d in ZS] for blocks, _, _ in rings]


def along_x(parts, sign):
    out = dict()
    for i, gate in ((0, None), (6, None), (7, None), (2, None), (4, None), (3, None), (5, 2), (1, 4)):
        dx, dc = SHIFTS[i]
        part = parts[i] if gate is None else after(parts[i], out[gate])
        out[i] = move(part, dx=sign * dx, dc=sign * dc)
    return [out[i] for i in range(len(SHIFTS))]


def on_device(tokens, out_grad, routes, gates, w_gate, w_up, w_down):
    rows, width = tokens.shape
    half, quarter, eighth = width // 2, width // 4, width // 8
    me = lax.axis_index("expert")
    y = lax.axis_index("etp")
    x, z, core = me // (NZ * NC), (me // NC) % NZ, me % NC
    side = y % 2
    wgate, wup, wdown = w_gate[0], w_up[0], w_down[0]

    first, second = prepare(y, tokens, out_grad, routes, gates)
    meta_end = quarter + 128
    first_z, second_z = gather_z(first, second)

    route_z = jnp.concatenate([b[:, quarter : quarter + 8] for b in first_z], axis=0).astype(F32)
    ids = jnp.stack(
        [((x + dx) % NX) * (NZ * NC) + z * NC + (core + dc) % NC for dx, dc in SHIFTS]
    ).astype(F32)
    hit = route_z[:, None, :] == ids[None, :, None]
    chosen = jnp.any(hit, axis=2).astype(F32)
    count = NZ * rows
    spot = jnp.arange(count, dtype=jnp.int32)
    before = ((spot[:, None] // rows == spot[None, :] // rows) & (spot[:, None] > spot[None, :])).astype(BF)
    position = dot(before, chosen.astype(BF))
    place = jnp.where(chosen > 0, position, -1.0).T
    slot = jnp.arange(BLOCK, dtype=jnp.int32)
    wanted = jnp.where(
        slot[:, None] // CAP == spot[None, :] // rows, (slot[:, None] % CAP).astype(F32), -2.0
    )
    picked = place[:, None, :] == wanted[None, :, :]
    picker = picked.astype(BF).reshape(len(SHIFTS) * BLOCK, count)

    def send_x_twice(parts, early):
        own = move(parts[0][BLOCK:], dc=1)
        near = [move(part, dx=dx) for part, dx in zip(parts[1:3], XS[1:3])]
        far = move(after(parts[3], *near), dx=XS[3])
        parts = [parts[0], *near, far]
        other = [part[BLOCK:] for part in parts]
        near = move(after(jnp.concatenate(other[1:3], axis=0), *early), dc=1)
        other = [own, near[:BLOCK], near[BLOCK:], move(other[3], dc=1)]
        pairs = [[part[:BLOCK], rest] for part, rest in zip(parts, other)]
        return jnp.concatenate(sum(pairs, []), axis=0)

    tok_rows = select(picker, [(first_z, 0, meta_end)], len(SHIFTS))
    tok_rows = [move(part, dx=dx, dc=dc) for part, (dx, dc) in zip(tok_rows, SHIFTS)]
    tok_x = jnp.concatenate(tok_rows, axis=0)
    tok_own, meta_x = tok_x[:, :quarter], tok_x[:, quarter : quarter + 16].astype(F32)
    tok_up, tok_down = move_y(tok_own, 1), move_y(tok_own, -1)
    tok_far_low, tok_far_high = move_y(tok_up[:, :eighth], 1), move_y(tok_down[:, eighth:], -1)
    pieces = [(first_z, meta_end, first.shape[1]), (second_z, 0, second.shape[1])]
    grad_rows = select(picker, [piece for piece in pieces if piece[1] < piece[2]], len(XS))
    gates_x = (tok_x, tok_rows[2], tok_rows[4], tok_x)
    grad_x = send_x_twice([after(part, gate) for part, gate in zip(grad_rows, gates_x)], (tok_up, tok_down))
    grad_low, grad_high = move_y(grad_x[:, :quarter], 1), move_y(grad_x[:, quarter:], -1)
    gate_vals = jnp.sum(
        jnp.where(meta_x[:, :8] == me.astype(F32), meta_x[:, 8:], 0.0), axis=1, keepdims=True
    )
    own_at, low_at = side * half, (1 - side) * half
    high_at = low_at + quarter
    far_at = ((y + 2) % NY) * quarter
    token_parts = (
        (tok_own, y * quarter),
        (tok_up, ((y - 1) % NY) * quarter),
        (tok_down, ((y + 1) % NY) * quarter),
        (tok_far_low, far_at),
        (tok_far_high, far_at + eighth),
    )

    def by_rows(weight):
        return sum(
            dot(part, lax.dynamic_slice_in_dim(weight, at, part.shape[1], 0))
            for part, at in token_parts
        )

    pre_gate = by_rows(wgate)
    pre_up = by_rows(wup)
    raw = dot_t(grad_x, lax.dynamic_slice_in_dim(wdown, own_at, half, 1))
    wgate, wup, wdown = [after(w, tok_up) for w in (wgate, wup, wdown)]
    wd_low, wd_high = [
        lax.dynamic_slice_in_dim(wdown, at, quarter, 1) for at in (low_at, high_at)
    ]

    def quarters(step):
        at = ((y + step) % NY) * quarter
        return [lax.dynamic_slice_in_dim(w, at, quarter, 0) for w in (wgate, wup)]

    grad_gate, grad_up, own_gate, far_up, far_down = backward(
        pre_gate, pre_up, raw, gate_vals, grad_low, grad_high, wd_low, wd_high, *quarters(2)
    )
    far_up, far_down = move_y(far_up, 1), move_y(far_down, -1)
    near = neighbours(grad_gate, grad_up, *quarters(1), *quarters(-1))
    up, down = forward(*near, far_up, far_down)
    up, down = move_y(up, 1), move_y(down, -1)
    mine = sum(dot_t(g, w) for g, w in zip((grad_gate, grad_up), quarters(0)))
    share = finish(mine, up, down, own_gate, far_up, far_down)
    back = along_x(share, -1)

    gate_back = jnp.stack([b[:, quarter : quarter + 1] for b in back]).astype(F32)
    by_expert = jnp.sum(jnp.where(picked, gate_back, 0.0), axis=1).T
    gate_tok = jnp.sum(jnp.where(hit, by_expert[:, :, None], 0.0), axis=1).astype(BF)
    gate_tok = jnp.concatenate([gate_tok, jnp.zeros((count, 120), BF)], axis=1)
    partial = combine(picker, gate_tok, back)
    arrived = [move(part, dz=-dz) for part, dz in zip(partial, ZS)]
    return tuple(total_of(arrived, routes.shape[1]))


def solution(mesh):
    return jax.shard_map(
        on_device,
        mesh=mesh,
        in_specs=(
            P("expert", None),
            P("expert", None),
            P("expert", None),
            P("expert", None),
            P("expert", None, "etp"),
            P("expert", None, "etp"),
            P("expert", "etp", None),
        ),
        out_specs=(P("expert", "etp"), P("expert", None)),
        check_vma=False,
    )
```

```python
import functools

import jax
import jax.numpy as jnp
from jax import lax
from jax.experimental import pallas as pl
from jax.experimental.pallas import tpu as pltpu
from jax.sharding import PartitionSpec as P

BF = jnp.bfloat16
F32 = jnp.float32
NX, NZ, NC, NY = 4, 8, 2, 4
CAP = 5
XS = (0, 1, -1, 2)
SHIFTS = tuple((dx, dc) for dx in XS for dc in (0, 1))
ZS = (0, 1, -1, 2, -2, 3, -3, 4)
BLOCK = NZ * CAP
VMEM = pl.BlockSpec(memory_space=pltpu.VMEM)


def params(mib):
    return pltpu.CompilerParams(vmem_limit_bytes=mib << 20)


def after(value, *others):
    return lax.optimization_barrier((value,) + others)[0]


def move(value, dx=0, dz=0, dc=0):
    if dx % NX == 0 and dz % NZ == 0 and dc % NC == 0:
        return value
    pairs = []
    for x in range(NX):
        for z in range(NZ):
            for c in range(NC):
                to = (((x + dx) % NX) * NZ + (z + dz) % NZ) * NC + (c + dc) % NC
                pairs.append(((x * NZ + z) * NC + c, to))
    return lax.ppermute(value, "expert", pairs)


def move_y(value, dy):
    return lax.ppermute(value, "etp", [(y, (y + dy) % NY) for y in range(NY)])


def prepare_kernel(at_ref, tok_ref, grad_ref, routes_ref, gates_ref, first_out, second_out, sems):
    half = tok_ref.shape[1] // 2
    quarter = half // 2
    start = quarter + 128
    more = first_out.shape[1] - start
    tok_at = pl.multiple_of(at_ref[0] * quarter, 128)
    grad_at = pl.multiple_of(lax.rem(at_ref[0], 2) * half, 128)
    copies = [
        (tok_ref.at[:, pl.ds(tok_at, quarter)], first_out.at[:, :quarter]),
        (grad_ref.at[:, pl.ds(grad_at + more, half - more)], second_out),
    ]
    if more:
        copies.append((grad_ref.at[:, pl.ds(grad_at, more)], first_out.at[:, start:]))
    copies = [pltpu.make_async_copy(*pair, sems.at[i]) for i, pair in enumerate(copies)]
    for copy in copies:
        copy.start()
    meta = jnp.concatenate([routes_ref[...].astype(F32), gates_ref[...].astype(F32)], axis=0)
    shape = (meta.shape[0], 128)
    unit = lax.broadcasted_iota(jnp.int32, shape, 0) == lax.broadcasted_iota(jnp.int32, shape, 1)
    meta = lax.dot_general(
        meta.astype(BF), unit.astype(BF), (((0,), (0,)), ((), ())), preferred_element_type=F32
    )
    first_out[:, quarter:start] = meta.astype(BF)
    for copy in copies:
        copy.wait()


def prepare(y, tokens, out_grad, routes, gates):
    rows, width = tokens.shape
    whole = width // 4 + 128 + width // 2
    first = max(whole // 256 * 128, width // 4 + 128)
    anywhere = pl.BlockSpec(memory_space=pl.ANY)
    return pl.pallas_call(
        prepare_kernel,
        out_shape=[jax.ShapeDtypeStruct((rows, size), BF) for size in (first, whole - first)],
        in_specs=[pl.BlockSpec(memory_space=pltpu.SMEM), anywhere, anywhere, VMEM, VMEM],
        out_specs=[VMEM] * 2,
        scratch_shapes=[pltpu.SemaphoreType.DMA((3,))],
        compiler_params=params(56),
    )(y.reshape(1), tokens, out_grad, routes.T, gates.T)


def total_kernel(*refs):
    blocks, (grad_out, gate_out) = refs[:NZ], refs[NZ:]
    width = grad_out.shape[1]
    total = blocks[0][...].astype(F32)
    for ref in blocks[1:]:
        total += ref[...].astype(F32)
    grad_out[...] = total[:, :width].astype(BF)
    gate_out[...] = total[:, width : width + gate_out.shape[1]].astype(BF)


def total_of(blocks, choices):
    rows, width = blocks[0].shape
    return pl.pallas_call(
        total_kernel,
        out_shape=[jax.ShapeDtypeStruct((rows, size), BF) for size in (width - 128, choices)],
        in_specs=[VMEM] * NZ,
        out_specs=[VMEM] * 2,
        compiler_params=params(8),
    )(*blocks)


def select_kernel(tile, pieces, picker_ref, *refs):
    count = len(pieces) * NZ
    outs = refs[count:]
    rows = outs[0].shape[0]
    target = 0
    for n, (first, last) in enumerate(pieces):
        blocks = refs[n * NZ : (n + 1) * NZ]

        def step(start, size, blocks=blocks, shift=target - first):
            part = jnp.concatenate([ref[:, pl.ds(start, size)] for ref in blocks], axis=0)
            found = jnp.dot(picker_ref[...], part, preferred_element_type=F32)
            for i, ref in enumerate(outs):
                ref[:, pl.ds(start + shift, size)] = found[i * rows : (i + 1) * rows].astype(BF)

        def body(i, carry, step=step, first=first):
            step(pl.multiple_of(first + i * tile, 128), tile)
            return carry

        lax.fori_loop(0, (last - first) // tile, body, 0)
        rest = (last - first) % tile
        if rest:
            step(last - rest, rest)
        target += last - first


def select(picker, pieces, count):
    rows = picker.shape[0] // count
    spans = tuple((first, last) for _, first, last in pieces)
    width = sum(last - first for first, last in spans)
    blocks = sum([blocks for blocks, _, _ in pieces], [])
    return pl.pallas_call(
        functools.partial(select_kernel, 512, spans),
        out_shape=[jax.ShapeDtypeStruct((rows, width), BF)] * count,
        in_specs=[VMEM] * (1 + len(blocks)),
        out_specs=[VMEM] * count,
        compiler_params=params(16),
        cost_estimate=pl.CostEstimate(
            flops=2 * picker.size * width, bytes_accessed=NZ * 104 * width * 2, transcendentals=0
        ),
    )(picker, *blocks)


def combine_kernel(tile, picker_ref, gate_ref, *refs):
    blocks, outs = refs[: len(SHIFTS)], refs[len(SHIFTS) :]
    width = blocks[0].shape[1]
    rows = outs[0].shape[0]

    def body(i, carry):
        columns = pl.ds(pl.multiple_of(i * tile, tile), tile)
        part = jnp.concatenate([ref[:, columns].astype(F32) for ref in blocks], axis=0).astype(BF)
        found = lax.dot_general(
            picker_ref[...], part, (((0,), (0,)), ((), ())), preferred_element_type=F32
        )
        for b, ref in enumerate(outs):
            ref[:, columns] = found[b * rows : (b + 1) * rows].astype(BF)
        return carry

    lax.fori_loop(0, (width - 128) // tile, body, 0)
    for b, ref in enumerate(outs):
        ref[:, width - 128 :] = gate_ref[b * rows : (b + 1) * rows]


def combine(picker, gate_tok, blocks):
    width = blocks[0].shape[1]
    rows = picker.shape[1] // NZ
    tile = 256 if (width - 128) % 256 == 0 else 128
    return pl.pallas_call(
        functools.partial(combine_kernel, tile),
        out_shape=[jax.ShapeDtypeStruct((rows, width), BF)] * NZ,
        in_specs=[VMEM] * (2 + len(SHIFTS)),
        out_specs=[VMEM] * NZ,
        compiler_params=params(16),
        cost_estimate=pl.CostEstimate(
            flops=2 * picker.size * width, bytes_accessed=NZ * 72 * width * 2, transcendentals=0
        ),
    )(picker, gate_tok, *blocks)


def dot(a, b):
    return jnp.dot(a, b, preferred_element_type=F32)


def dot_t(a, b):
    return lax.dot_general(a, b, (((1,), (1,)), ((), ())), preferred_element_type=F32)


def backward_kernel(*refs):
    gate_ref, up_ref, raw_ref, scale_ref, low_ref, high_ref = refs[:6]
    wd_low, wd_high, wg_far, wu_far = refs[6:10]
    gg_out, gu_out, own_out, far_up, far_down = refs[10:]
    eighth = far_up.shape[1] - 128
    pre_gate, pre_up = gate_ref[...], up_ref[...]
    raw = raw_ref[...] + dot_t(low_ref[...], wd_low[...]) + dot_t(high_ref[...], wd_high[...])
    sigma = jax.nn.sigmoid(pre_gate)
    silu_val = pre_gate * sigma
    act = (silu_val * pre_up).astype(BF)
    rest = jnp.sum(act.astype(F32) * raw, axis=1, keepdims=True)
    grad_act = raw * scale_ref[...]
    grad_gate = (grad_act * pre_up * sigma * (1.0 + pre_gate * (1.0 - sigma))).astype(BF)
    grad_up = (grad_act * silu_val).astype(BF)
    gg_out[...] = grad_gate
    gu_out[...] = grad_up
    lane = lax.broadcasted_iota(jnp.int32, own_out.shape, 1)
    columns = jnp.zeros(own_out.shape, F32)
    for i in range(3):
        piece = rest.astype(BF).astype(F32)
        columns = jnp.where(lane == i, piece, columns)
        rest = rest - piece
    columns = columns.astype(BF)
    own_out[...] = columns
    for out, at in ((far_up, 0), (far_down, eighth)):
        rows = slice(at, at + eighth)
        far = dot_t(grad_gate, wg_far[rows, :]) + dot_t(grad_up, wu_far[rows, :])
        out[:, :eighth] = far.astype(BF)
        out[:, eighth:] = columns


def backward(*args):
    rows, hidden = args[0].shape
    eighth = args[4].shape[1] // 2
    shape = jax.ShapeDtypeStruct
    return pl.pallas_call(
        backward_kernel,
        out_shape=(
            [shape((rows, hidden), BF)] * 2
            + [shape((rows, 128), BF)]
            + [shape((rows, eighth + 128), BF)] * 2
        ),
        in_specs=[VMEM] * len(args),
        out_specs=[VMEM] * 5,
        compiler_params=params(32),
    )(*args)


def neighbours_kernel(gg_ref, gu_ref, wg_up, wu_up, wg_down, wu_down, *outs):
    up_low, up_high, down_low, down_high = outs
    eighth = up_low.shape[1]
    gg, gu = gg_ref[...], gu_ref[...]
    for wg, wu, low, high in ((wg_up, wu_up, up_low, up_high), (wg_down, wu_down, down_low, down_high)):
        for out, at in ((low, 0), (high, eighth)):
            rows = slice(at, at + eighth)
            out[...] = (dot_t(gg, wg[rows, :]) + dot_t(gu, wu[rows, :])).astype(out.dtype)


def neighbours(*args):
    rows, eighth = args[0].shape[0], args[2].shape[0] // 2
    kinds = (F32, BF, BF, F32)
    return pl.pallas_call(
        neighbours_kernel,
        out_shape=[jax.ShapeDtypeStruct((rows, eighth), kind) for kind in kinds],
        in_specs=[VMEM] * len(args),
        out_specs=[VMEM] * 4,
        compiler_params=params(32),
    )(*args)


def forward_kernel(up_low, up_high, down_low, down_high, far_up, far_down, up, down):
    eighth = up_low.shape[1]
    up[:, :eighth] = (up_low[...] + far_up[:, :eighth].astype(F32)).astype(BF)
    up[:, eighth : 2 * eighth] = up_high[...]
    up[:, 2 * eighth :] = far_up[:, eighth:]
    down[:, :eighth] = down_low[...]
    down[:, eighth:] = (down_high[...] + far_down[:, :eighth].astype(F32)).astype(BF)


def forward(*args):
    rows, eighth = args[0].shape
    return pl.pallas_call(
        forward_kernel,
        out_shape=[jax.ShapeDtypeStruct((rows, 2 * eighth + more), BF) for more in (128, 0)],
        in_specs=[VMEM] * len(args),
        out_specs=[VMEM] * 2,
        compiler_params=params(32),
    )(*args)


def finish_kernel(mine, up, down, own, far_up, far_down, *outs):
    quarter = mine.shape[1]
    gate = [
        jnp.sum(ref[:, ref.shape[1] - 128 :].astype(F32), axis=1, keepdims=True)
        for ref in (own, up, far_up, far_down)
    ]
    slot_gate = (gate[0] + gate[1]) + (gate[2] + gate[3])
    lane = lax.broadcasted_iota(jnp.int32, own.shape, 1)
    extra = jnp.where(lane == 0, slot_gate, 0.0)
    for at in range(0, quarter, 128):
        columns = slice(at, at + 128)
        total = mine[:, columns] + up[:, columns].astype(F32) + down[:, columns].astype(F32)
        for i, ref in enumerate(outs):
            ref[:, columns] = total[i * BLOCK : (i + 1) * BLOCK].astype(BF)
    for i, ref in enumerate(outs):
        ref[:, quarter:] = extra[i * BLOCK : (i + 1) * BLOCK].astype(BF)


def finish(mine, *args):
    return pl.pallas_call(
        finish_kernel,
        out_shape=[jax.ShapeDtypeStruct((BLOCK, mine.shape[1] + 128), BF)] * len(SHIFTS),
        in_specs=[VMEM] * (1 + len(args)),
        out_specs=[VMEM] * len(SHIFTS),
        compiler_params=params(32),
    )(mine, *args)


def gather_z(first, second):
    rings = [({0: value}, value, value) for value in (first, second)]
    for step in range(1, 5):
        for n, (blocks, up, down) in enumerate(rings):
            if step < 4 or n == 0:
                up = blocks[step] = move(up, dz=1)
            if step < 4 or n == 1:
                down = move(down, dz=-1)
                blocks[-step if step < 4 else step] = down
            rings[n] = (blocks, up, down)
    return [[blocks[d] for d in ZS] for blocks, _, _ in rings]


def along_x(parts, sign):
    out = dict()
    for i, gate in ((0, None), (6, None), (7, None), (2, None), (4, None), (3, None), (5, 2), (1, 4)):
        dx, dc = SHIFTS[i]
        part = parts[i] if gate is None else after(parts[i], out[gate])
        out[i] = move(part, dx=sign * dx, dc=sign * dc)
    return [out[i] for i in range(len(SHIFTS))]


def on_device(tokens, out_grad, routes, gates, w_gate, w_up, w_down):
    rows, width = tokens.shape
    half, quarter, eighth = width // 2, width // 4, width // 8
    me = lax.axis_index("expert")
    y = lax.axis_index("etp")
    x, z, core = me // (NZ * NC), (me // NC) % NZ, me % NC
    side = y % 2
    wgate, wup, wdown = w_gate[0], w_up[0], w_down[0]

    first, second = prepare(y, tokens, out_grad, routes, gates)
    meta_end = quarter + 128
    first_z, second_z = gather_z(first, second)

    route_z = jnp.concatenate([b[:, quarter : quarter + 8] for b in first_z], axis=0).astype(F32)
    ids = jnp.stack(
        [((x + dx) % NX) * (NZ * NC) + z * NC + (core + dc) % NC for dx, dc in SHIFTS]
    ).astype(F32)
    hit = route_z[:, None, :] == ids[None, :, None]
    chosen = jnp.any(hit, axis=2).astype(F32)
    count = NZ * rows
    spot = jnp.arange(count, dtype=jnp.int32)
    before = ((spot[:, None] // rows == spot[None, :] // rows) & (spot[:, None] > spot[None, :])).astype(BF)
    position = dot(before, chosen.astype(BF))
    place = jnp.where(chosen > 0, position, -1.0).T
    slot = jnp.arange(BLOCK, dtype=jnp.int32)
    wanted = jnp.where(
        slot[:, None] // CAP == spot[None, :] // rows, (slot[:, None] % CAP).astype(F32), -2.0
    )
    picked = place[:, None, :] == wanted[None, :, :]
    picker = picked.astype(BF).reshape(len(SHIFTS) * BLOCK, count)

    def send_x_twice(parts, early):
        own = move(parts[0][BLOCK:], dc=1)
        near = [move(part, dx=dx) for part, dx in zip(parts[1:3], XS[1:3])]
        far = move(after(parts[3], *near), dx=XS[3])
        parts = [parts[0], *near, far]
        other = [part[BLOCK:] for part in parts]
        near = move(after(jnp.concatenate(other[1:3], axis=0), *early), dc=1)
        other = [own, near[:BLOCK], near[BLOCK:], move(other[3], dc=1)]
        pairs = [[part[:BLOCK], rest] for part, rest in zip(parts, other)]
        return jnp.concatenate(sum(pairs, []), axis=0)

    tok_rows = select(picker, [(first_z, 0, meta_end)], len(SHIFTS))
    tok_rows = [move(part, dx=dx, dc=dc) for part, (dx, dc) in zip(tok_rows, SHIFTS)]
    tok_x = jnp.concatenate(tok_rows, axis=0)
    tok_own, meta_x = tok_x[:, :quarter], tok_x[:, quarter : quarter + 16].astype(F32)
    tok_up, tok_down = move_y(tok_own, 1), move_y(tok_own, -1)
    tok_far_low, tok_far_high = move_y(tok_up[:, :eighth], 1), move_y(tok_down[:, eighth:], -1)
    pieces = [(first_z, meta_end, first.shape[1]), (second_z, 0, second.shape[1])]
    grad_rows = select(picker, [piece for piece in pieces if piece[1] < piece[2]], len(XS))
    gates_x = (tok_x, tok_rows[2], tok_rows[4], tok_x)
    grad_x = send_x_twice([after(part, gate) for part, gate in zip(grad_rows, gates_x)], (tok_up, tok_down))
    grad_low, grad_high = move_y(grad_x[:, :quarter], 1), move_y(grad_x[:, quarter:], -1)
    gate_vals = jnp.sum(
        jnp.where(meta_x[:, :8] == me.astype(F32), meta_x[:, 8:], 0.0), axis=1, keepdims=True
    )
    own_at, low_at = side * half, (1 - side) * half
    high_at = low_at + quarter
    far_at = ((y + 2) % NY) * quarter
    token_parts = (
        (tok_own, y * quarter),
        (tok_up, ((y - 1) % NY) * quarter),
        (tok_down, ((y + 1) % NY) * quarter),
        (tok_far_low, far_at),
        (tok_far_high, far_at + eighth),
    )

    def by_rows(weight):
        return sum(
            dot(part, lax.dynamic_slice_in_dim(weight, at, part.shape[1], 0))
            for part, at in token_parts
        )

    pre_gate = by_rows(wgate)
    pre_up = by_rows(wup)
    raw = dot_t(grad_x, lax.dynamic_slice_in_dim(wdown, own_at, half, 1))
    wgate, wup, wdown = [after(w, tok_up) for w in (wgate, wup, wdown)]
    wd_low, wd_high = [
        lax.dynamic_slice_in_dim(wdown, at, quarter, 1) for at in (low_at, high_at)
    ]

    def quarters(step):
        at = ((y + step) % NY) * quarter
        return [lax.dynamic_slice_in_dim(w, at, quarter, 0) for w in (wgate, wup)]

    grad_gate, grad_up, own_gate, far_up, far_down = backward(
        pre_gate, pre_up, raw, gate_vals, grad_low, grad_high, wd_low, wd_high, *quarters(2)
    )
    far_up, far_down = move_y(far_up, 1), move_y(far_down, -1)
    near = neighbours(grad_gate, grad_up, *quarters(1), *quarters(-1))
    up, down = forward(*near, far_up, far_down)
    up, down = move_y(up, 1), move_y(down, -1)
    mine = sum(dot_t(g, w) for g, w in zip((grad_gate, grad_up), quarters(0)))
    share = finish(mine, up, down, own_gate, far_up, far_down)
    back = along_x(share, -1)

    gate_back = jnp.stack([b[:, quarter : quarter + 1] for b in back]).astype(F32)
    by_expert = jnp.sum(jnp.where(picked, gate_back, 0.0), axis=1).T
    gate_tok = jnp.sum(jnp.where(hit, by_expert[:, :, None], 0.0), axis=1).astype(BF)
    gate_tok = jnp.concatenate([gate_tok, jnp.zeros((count, 120), BF)], axis=1)
    partial = combine(picker, gate_tok, back)
    arrived = [move(part, dz=-dz) for part, dz in zip(partial[::-1], ZS[::-1])]
    return tuple(total_of(arrived, routes.shape[1]))


def solution(mesh):
    return jax.shard_map(
        on_device,
        mesh=mesh,
        in_specs=(
            P("expert", None),
            P("expert", None),
            P("expert", None),
            P("expert", None),
            P("expert", None, "etp"),
            P("expert", None, "etp"),
            P("expert", "etp", None),
        ),
        out_specs=(P("expert", "etp"), P("expert", None)),
        check_vma=False,
    )
```
